32 devices in a mesh: groups: 2 (over y), band: 4 (over z), lev: 2 (over x), rd: 2 (over core).
Axes of the slice: x: 2, y: 2, z: 4, core: 2. Of those that a mesh axis runs over, the one named last changes fastest.
Arguments:
- departures: bfloat16 [2048, 8, 128], P(('groups', 'band', 'rd'), 'lev'), parts along dimension 0, may hold values from -6 to 6
- destinations: int32 [2048, 1], P(('groups', 'band', 'rd')), parts along dimension 0, may hold values from 0 to 3; in each aligned block of 128 rows (0 to 127, 128 to 255, ...) at most 64 rows name the same one
- tile_index: int32 [2048], P(('groups', 'band', 'rd')), parts along dimension 0, may hold values from 0 to 895
- obs_count: int32 [2048], P(('groups', 'band', 'rd')), parts along dimension 0, may hold values from 1 to 128
- interp_weights: bfloat16 [2048, 128, 128], P(('groups', 'band', 'rd')), parts along dimension 0, may hold values from -0.5 to 0.5
- background: float32 [16, 64, 7168], P(('groups', 'lev', 'rd'), 'band'), parts along dimension 0, may hold values from -6 to 6
- lon_taps: float32 [17, 7168], replicated, may hold values from 0.1 to 0.5
- lat_taps: float32 [17, 64], replicated, may hold values from 0.1 to 0.5
Outputs:
- filtered: float32 [16, 64, 7168], P(('groups', 'lev', 'rd'), 'band'), parts along dimension 0
The draws below stay inside these ranges and needn't reach their ends.
There are 2 independent parts, one for each index of `groups`. The reference program is written for one: setup_inputs(seed, part) draws one part's arguments, and reference() takes and returns one part's arrays. A program takes and returns all parts, laid end to end along the dimension named above; an argument that names none is the same for every part. Nothing has to cross between parts.
Inputs may be any that keep to these rules, and one draw needn't show every extreme that they name: `destinations`: among the 128 blocks of one reader device, no band is named by more than 64 blocks.
All inputs are finite; a program needn't handle non-finite values.
Results may differ from the reference program's by a relative error of at most 0.0003.
Values sent between devices are 32-bit elements; how exact they have to be, the bound alone decides.
A program may use at most 64 MiB of HBM per device.

```python
import math
import jax
import jax.numpy as jnp
import numpy as np
from jax import lax

NLON = 7168
OBS = 128
TILE = 128
REACH = 8
BLK_DEV = 128
CAP = 64
BLOCKS = 1024
SLABS = 8
NLAT = 64
TILES = 896
TAPS = 17
N_BAND = 4


def plant(entries, own_key, low, largest):
    shape = entries.shape
    index_at = [jax.random.randint(jax.random.fold_in(own_key, axis), (), 0, shape[axis]) for axis in range(len(shape))]
    entries = entries.at[tuple(index_at)].set(low)
    longest = shape.index(max(shape))
    index_at[longest] = (index_at[longest] + 1) % shape[longest]
    return entries.at[tuple(index_at)].set(largest)


def block_scale(rng, extent, shards, least, top_value):
    def one(axis_at, parts):
        steps = jax.random.uniform(jax.random.fold_in(jax.random.fold_in(rng, 6), axis_at), (parts,), jnp.float32, least / len(shards), top_value / len(shards))
        return jnp.repeat(jnp.exp(steps), extent[axis_at] // parts).reshape((-1,) + (1,) * (len(extent) - axis_at - 1))

    level = one(*shards[0])
    for cut in shards[1:]:
        level = level * one(*cut)
    return level


def routed_block(stream_key, own, number, rows, number_of, top, bound, skew):
    sequence = jax.random.permutation(stream_key, number_of)
    crowded, usual = portions_of(number_of, rows * top, bound, skew, True), portions_of(number_of, rows * top, bound, skew, False)
    places = jnp.arange(number_of)

    def named(lengths, rotation):
        used = int((lengths > 0).sum())
        fixed = max(1, used // 4)
        shifted = fixed + (places - fixed + rotation * (used - fixed)) % max(1, number_of - fixed)
        return jnp.zeros((number_of,), jnp.int32).at[sequence[jnp.where(places < fixed, places, shifted)]].set(jnp.asarray(lengths, jnp.int32))

    lengths = jnp.where(number % 4 == 0, named(crowded, number // 4), named(usual, number - number // 4 - 1))
    mixed = jax.random.permutation(jax.random.fold_in(own, 3), number_of)
    source_of, sink = mixed[0:number_of // 2 * 2:2], mixed[1:number_of // 2 * 2:2]
    slack = jnp.minimum(lengths[source_of] - 1, bound - lengths[sink]) // 2
    slack = jnp.where((source_of == sequence[0]) | (sink == sequence[0]) | (lengths[sink] == 0), 0, jnp.maximum(slack, 0))
    shifted = jax.random.randint(jax.random.fold_in(own, 4), (number_of // 2,), 0, 1 << 20) % (slack + 1)
    lengths = lengths.at[source_of].add(-shifted).at[sink].add(shifted)
    labels = jnp.searchsorted(jnp.cumsum(lengths), jnp.arange(rows * top), side="right").astype(jnp.int32)
    grid = labels.reshape(top, rows).T
    grid = grid[jax.random.permutation(jax.random.fold_in(own, 1), rows)]
    rotation = jax.random.randint(jax.random.fold_in(own, 2), (rows, 1), 0, top)
    return jnp.take_along_axis(grid, (jnp.arange(top)[None, :] + rotation) % top, axis=1)


def portions_of(number_of, total, reach, lean, full):
    loads = [(1 << 20) // math.isqrt(grade ** lean) + 1 for grade in range(1, number_of + 1)]
    largest = reach if full else min(reach, max(-(-total // number_of), total * loads[0] // sum(loads)))
    least = 1 if total - largest >= number_of - 1 else 0
    given, spare = [largest] + [least] * (number_of - 1), total - largest - least * (number_of - 1)
    while spare > 0:
        movable = [i for i in range(1, number_of) if given[i] < largest] or [i for i in range(1, number_of) if given[i] < reach]
        pool, budget = sum([loads[i] for i in movable]), spare
        for i in movable:
            more = min(reach - given[i], max(1, budget * loads[i] // pool), spare)
            given[i] = given[i] + more
            spare = spare - more
    return np.array(given)


def bell_draw(stream_key, extent, scale, reach, cuts=(), kind=jnp.bfloat16):
    drawn = jax.random.normal(stream_key, extent, jnp.float32) * scale
    if len(cuts) > 0:
        drawn = block_scale(stream_key, extent, cuts, -0.22, 0.18) * drawn
    return jnp.clip(drawn, min=-reach, max=reach).astype(kind)


def setup_inputs(seed: int = 0, part: int = 0) -> dict:
    streams_of = jax.random.split(jax.random.key(seed), 9)
    part_keys = jax.random.split(jax.random.fold_in(streams_of[8], part), 9)
    departures = bell_draw(part_keys[0], (BLOCKS, SLABS, OBS), 1.0, 6.0, ((0, 8), (1, 2)))
    destinations_keys = jax.random.split(jax.random.fold_in(part_keys[1], 1), BLOCKS // BLK_DEV)
    destinations_turns = jax.random.permutation(jax.random.fold_in(part_keys[1], 3), BLOCKS // BLK_DEV)
    destinations = jax.vmap(lambda own, number: routed_block(jax.random.fold_in(part_keys[1], 2), own, number, BLK_DEV, N_BAND, 1, CAP, 2))(destinations_keys, destinations_turns).reshape((BLOCKS, 1))
    tile_index = plant(jax.random.randint(part_keys[2], (BLOCKS,), 0, TILES), jax.random.fold_in(part_keys[2], 1), 0, TILES - 1).astype(jnp.int32)
    obs_count = plant(jax.random.randint(part_keys[3], (BLOCKS,), 1, OBS + 1), jax.random.fold_in(part_keys[3], 1), 1, OBS).astype(jnp.int32)
    interp_weights = bell_draw(part_keys[4], (BLOCKS, OBS, TILE), OBS ** -0.5, 0.5, ((0, 8),))
    background = bell_draw(part_keys[5], (SLABS, NLAT, NLON), 1.0, 6.0, ((0, 4), (1, 4)), jnp.float32)
    lon_taps = jnp.clip(jnp.exp(jax.random.uniform(streams_of[6], (TAPS, NLON), jnp.float32, math.log(0.1), math.log(0.5))), 0.1, 0.5)
    lat_taps = jnp.clip(jnp.exp(jax.random.uniform(streams_of[7], (TAPS, NLAT), jnp.float32, math.log(0.1), math.log(0.5))), 0.1, 0.5)
    return dict(departures=departures, destinations=destinations, tile_index=tile_index, obs_count=obs_count, interp_weights=interp_weights, background=background, lon_taps=lon_taps, lat_taps=lat_taps)


def reference(departures, destinations, tile_index, obs_count, interp_weights, background, lon_taps, lat_taps):
    positions = jnp.arange(OBS, dtype=jnp.int32)
    retained = (positions[None, :] < obs_count[:, None]).astype(jnp.float32)
    masked = departures.astype(jnp.float32) * retained[:, None, :]
    values = jnp.einsum("bso,boc->sbc", masked, interp_weights.astype(jnp.float32), precision=lax.Precision.HIGHEST)
    flat_index = (destinations[:, 0] * TILES + tile_index).astype(jnp.int32)
    increment = jnp.zeros((SLABS, N_BAND * TILES, TILE), jnp.float32).at[:, flat_index, :].add(values)
    summed = background + increment.reshape(SLABS, NLAT, NLON)
    padded = jnp.concatenate([summed[:, :, NLON - REACH:], summed, summed[:, :, :REACH]], axis=2)
    along_lon = jnp.zeros((SLABS, NLAT, NLON), jnp.float32)
    for offset in range(2 * REACH + 1):
        along_lon = along_lon + lon_taps[offset][None, None, :] * padded[:, :, offset:offset + NLON]
    padded = jnp.pad(along_lon, ((0, 0), (REACH, REACH), (0, 0)))
    filtered = jnp.zeros((SLABS, NLAT, NLON), jnp.float32)
    for offset in range(2 * REACH + 1):
        filtered = filtered + lat_taps[offset][None, :, None] * padded[:, offset:offset + NLAT, :]
    return filtered
```

```python
import functools

import jax
import jax.numpy as jnp
from jax import lax
from jax.experimental import pallas as pl
from jax.experimental.pallas import tpu as pltpu
from jax.sharding import PartitionSpec as P

NLON = 7168
OBS = 128
TILE = 128
REACH = 8
SLAB_DEV = 2
LAT_DEV = 16
BLK_DEV = 128
ROW_TILES = NLON // TILE
TILES = ROW_TILES * LAT_DEV
TAPS = 2 * REACH + 1
SPAN = LAT_DEV + 2 * REACH
W_PARTS = 4
CHUNK_TILES = 7
CHUNK = CHUNK_TILES * TILE
CHUNKS = NLON // CHUNK
F32 = jnp.float32
BF16 = jnp.bfloat16
MESH = pl.DeviceIdType.MESH


def iota(shape, axis):
    return lax.broadcasted_iota(jnp.int32, shape, axis)


def split(value):
    high = value.astype(BF16)
    return high, (value - high.astype(F32)).astype(BF16)


def kernel(
    n_band,
    n_rd,
    cap,
    dep_ref,
    dest_ref,
    tile_ref,
    count_ref,
    w_hbm,
    bg_hbm,
    lon_hbm,
    lat_ref,
    out_hbm,
    w_v,
    values,
    outbox,
    inbox,
    onehot,
    field,
    along,
    lon_v,
    out_v,
    w_sem,
    bg_sem,
    lon_sem,
    out_sem,
    box_send,
    box_recv,
    halo_send,
    halo_recv,
):
    n_src = n_band * n_rd
    slots = n_band * cap
    per_group = TILE // cap
    groups = n_src // per_group
    band = lax.axis_index("band")
    rd = lax.axis_index("rd")
    me = band * n_rd + rd

    w_copies = []
    part = BLK_DEV // W_PARTS
    for i in range(W_PARTS):
        rows = pl.ds(i * part, part)
        w_copies.append(pltpu.make_async_copy(w_hbm.at[rows], w_v.at[rows], w_sem.at[i]))
        w_copies[-1].start()
    bg_copies = []
    for s in range(SLAB_DEV):
        bg_copies.append(
            pltpu.make_async_copy(
                bg_hbm.at[s], field.at[s, :, pl.ds(TILE, NLON)], bg_sem.at[s]
            )
        )
        bg_copies[-1].start()
    lon_copy = pltpu.make_async_copy(lon_hbm, lon_v, lon_sem)
    lon_copy.start()

    barrier = pltpu.get_barrier_semaphore()

    def greet(step, carry):
        other = lax.rem(me + step, n_src)
        pl.semaphore_signal(
            barrier,
            inc=1,
            device_id={"band": other // n_rd, "rd": lax.rem(other, n_rd)},
            device_id_type=MESH,
        )
        return carry

    lax.fori_loop(1, n_src, greet, 0)

    square = (BLK_DEV, BLK_DEV)
    lane, sub = iota(square, 1), iota(square, 0)
    eye = lane == sub
    dest = jnp.broadcast_to(dest_ref[...], square)
    chosen = (dest == lane).astype(F32)
    before = (lane < sub).astype(BF16)
    earlier = jnp.dot(before, chosen.astype(BF16), preferred_element_type=F32)
    rank = jnp.sum(earlier * chosen, axis=1, keepdims=True)
    slot = dest_ref[...].astype(F32) * cap + rank
    slot_row = jnp.sum(jnp.where(eye, slot, 0.0), axis=0, keepdims=True)
    pack = (iota((slots, BLK_DEV), 0).astype(F32) == slot_row).astype(BF16)
    tile_row = tile_ref[...]
    lat_row = jnp.zeros_like(tile_row)
    for r in range(1, LAT_DEV):
        lat_row = lat_row + (tile_row >= r * ROW_TILES).astype(jnp.int32)
    place_row = (tile_row - lat_row * ROW_TILES) * LAT_DEV + lat_row + 1
    place = jnp.sum(jnp.where(eye, place_row.astype(F32), 0.0), axis=1, keepdims=True)
    shift = lax.rem(me, per_group) * cap
    lane_at = (lane - shift).astype(F32)
    label_of = jnp.where(lane_at == rank, place, 0.0)
    for d in range(n_band):
        row = jnp.sum(jnp.where(dest == d, label_of, 0.0), axis=0, keepdims=True)
        row = jnp.broadcast_to(row, (8, TILE))
        for r in range(n_rd):
            outbox[0, d * n_rd + r, pl.ds(cap, 8), :] = row

    lanes4 = iota((2 * SLAB_DEV, OBS), 1)
    for i in range(W_PARTS):
        w_copies[i].wait()

        def multiply(pair, carry, i=i):
            both = []
            for h in range(2):
                b = i * part + pair * 2 + h
                obs = jnp.where(lanes4 < count_ref[b], dep_ref[b].astype(F32), 0.0)
                both.append(jnp.dot(obs.astype(BF16), w_v[b], preferred_element_type=F32))
            at = pl.multiple_of((i * (part // 2) + pair) * 8, 8)
            values[pl.ds(at, 8), :] = jnp.concatenate(both, axis=0)
            return carry

        lax.fori_loop(0, part // 2, multiply, 0, unroll=8)

    pl.semaphore_wait(barrier, n_src - 1)

    def box_copy(s, step):
        other = lax.rem(me + step, n_src)
        size = cap + 8 if s == 0 else cap
        return pltpu.make_async_remote_copy(
            src_ref=outbox.at[s, other, pl.ds(0, size)],
            dst_ref=inbox.at[s, me, pl.ds(0, size)],
            send_sem=box_send.at[s, step],
            recv_sem=box_recv.at[s, step],
            device_id={"band": other // n_rd, "rd": lax.rem(other, n_rd)},
            device_id_type=MESH,
        )

    for s in range(SLAB_DEV):
        for r in range(n_rd):
            value = values[pl.ds(r * SLAB_DEV + s, BLK_DEV, stride=2 * SLAB_DEV), :]
            both = jnp.dot(
                pack, jnp.concatenate(split(value), axis=1), preferred_element_type=F32
            )
            both = both[:, :TILE] + both[:, TILE:]
            for d in range(n_band):
                outbox[s, d * n_rd + r, pl.ds(0, cap), :] = both[d * cap : (d + 1) * cap]

        def send(step, carry, s=s):
            box_copy(s, step).start()
            return carry

        lax.fori_loop(1, n_src, send, 0)
        inbox[s, me] = outbox[s, me]

    n_lat = lat_ref.shape[1]
    wide = (LAT_DEV, 128)
    own = iota((LAT_DEV, n_lat), 1) == iota((LAT_DEV, n_lat), 0) + band * LAT_DEV
    lane16, sub16 = iota(wide, 1), iota(wide, 0)
    third = lane16 // SPAN
    offset = lane16 - third * SPAN - sub16
    lat_matrix = jnp.zeros(wide, F32)
    for k in range(TAPS):
        column = jnp.sum(jnp.where(own, lat_ref[k : k + 1, :], 0.0), axis=1, keepdims=True)
        lat_matrix = lat_matrix + jnp.where(offset == k, column, 0.0)
    high = lat_matrix.astype(BF16).astype(F32)
    lat_matrix = jnp.where(third == 1, lat_matrix - high, high).astype(BF16)[:, : 3 * SPAN]

    @pl.when(band == 0)
    def _():
        along[:, pl.ds(0, REACH), :] = jnp.zeros((SLAB_DEV, REACH, NLON), F32)

    @pl.when(band == n_band - 1)
    def _():
        along[:, pl.ds(REACH + LAT_DEV, REACH), :] = jnp.zeros((SLAB_DEV, REACH, NLON), F32)

    def halo_copy(s, up):
        source = LAT_DEV if up else REACH
        target = 0 if up else REACH + LAT_DEV
        return pltpu.make_async_remote_copy(
            src_ref=along.at[s, pl.ds(source, REACH)],
            dst_ref=along.at[s, pl.ds(target, REACH)],
            send_sem=halo_send.at[s, int(up)],
            recv_sem=halo_recv.at[s, int(up)],
            device_id={"band": band + 1 if up else band - 1, "rd": rd},
            device_id_type=MESH,
        )

    for s in range(SLAB_DEV):

        def take(step, carry, s=s):
            box_copy(s, step).wait_recv()
            return carry

        bg_copies[s].wait()
        lax.fori_loop(1, n_src, take, 0)
        if s == 0:
            rows = iota((CHUNK_TILES * LAT_DEV, TILE), 0) + 1
            for g in range(groups):
                label = jnp.sum(
                    inbox[0, pl.ds(g * per_group, per_group), cap, :], axis=0, keepdims=True
                )

                def mark(c, carry, g=g, label=label):
                    at = pl.multiple_of(c * CHUNK_TILES * LAT_DEV, 16)
                    hit = (rows + at).astype(F32) == label
                    onehot[pl.ds(at, CHUNK_TILES * LAT_DEV), pl.ds(g * TILE, TILE)] = hit.astype(
                        F32
                    ).astype(BF16)
                    return carry

                lax.fori_loop(0, CHUNKS, mark, 0)
            lon_copy.wait()
        received = inbox[s, :, pl.ds(0, cap), :].reshape(n_src * cap, TILE)
        pieces = jnp.concatenate(split(received), axis=1)

        def add(c, carry, s=s, pieces=pieces):
            at = pl.multiple_of(c * CHUNK_TILES * LAT_DEV, 16)
            both = jnp.dot(
                onehot[pl.ds(at, CHUNK_TILES * LAT_DEV), :], pieces, preferred_element_type=F32
            )
            both = both[:, :TILE] + both[:, TILE:]
            for q in range(CHUNK_TILES):
                columns = pl.ds(pl.multiple_of((c * CHUNK_TILES + q + 1) * TILE, TILE), TILE)
                field[s, :, columns] += both[q * LAT_DEV : (q + 1) * LAT_DEV]
            return carry

        lax.fori_loop(0, CHUNKS, add, 0)
        field[s, :, pl.ds(0, TILE)] = field[s, :, pl.ds(NLON, TILE)]
        field[s, :, pl.ds(NLON + TILE, TILE)] = field[s, :, pl.ds(TILE, TILE)]

        def lon_filter(c, carry, s=s):
            at = pl.multiple_of(c * CHUNK, TILE)
            width = CHUNK + 2 * TILE
            window = field[s, :, pl.ds(at, width)]
            total = jnp.zeros((LAT_DEV, CHUNK), F32)
            for k in range(TAPS):
                moved = window if k == REACH else pltpu.roll(window, (REACH - k) % width, 1)
                total = total + lon_v[k : k + 1, pl.ds(at, CHUNK)] * moved[:, TILE : TILE + CHUNK]
            along[s, pl.ds(REACH, LAT_DEV), pl.ds(at, CHUNK)] = total
            return carry

        lax.fori_loop(0, CHUNKS, lon_filter, 0)

        @pl.when(band < n_band - 1)
        def _(s=s):
            halo_copy(s, True).start()

        @pl.when(band > 0)
        def _(s=s):
            halo_copy(s, False).start()

    out_copies = []
    for s in range(SLAB_DEV):

        @pl.when(band > 0)
        def _(s=s):
            halo_copy(s, True).wait_recv()

        @pl.when(band < n_band - 1)
        def _(s=s):
            halo_copy(s, False).wait_recv()

        def lat_filter(c, carry, s=s):
            columns = pl.ds(pl.multiple_of(c * CHUNK, TILE), CHUNK)
            high, low = split(along[s, :, columns])
            out_v[s, :, columns] = jnp.dot(
                lat_matrix,
                jnp.concatenate([high, high, low], axis=0),
                preferred_element_type=F32,
            )
            return carry

        lax.fori_loop(0, CHUNKS, lat_filter, 0)
        out_copies.append(pltpu.make_async_copy(out_v.at[s], out_hbm.at[s], out_sem.at[s]))
        out_copies[-1].start()

    for s in range(SLAB_DEV):

        def sent(step, carry, s=s):
            box_copy(s, step).wait_send()
            return carry

        lax.fori_loop(1, n_src, sent, 0)

        @pl.when(band < n_band - 1)
        def _(s=s):
            halo_copy(s, True).wait_send()

        @pl.when(band > 0)
        def _(s=s):
            halo_copy(s, False).wait_send()

        out_copies[s].wait()


def on_device(
    departures, destinations, tile_index, obs_count, interp_weights, background, lon_taps, lat_taps
):
    n_band = lax.axis_size("band")
    n_rd = lax.axis_size("rd")
    cap = max(2, 2 * BLK_DEV // n_band)
    n_src = n_band * n_rd
    vmem = pl.BlockSpec(memory_space=pltpu.VMEM)
    hbm = pl.BlockSpec(memory_space=pl.ANY)
    dma = pltpu.SemaphoreType.DMA
    return pl.pallas_call(
        functools.partial(kernel, n_band, n_rd, cap),
        out_shape=jax.ShapeDtypeStruct(background.shape, F32),
        in_specs=[
            vmem,
            vmem,
            vmem,
            pl.BlockSpec(memory_space=pltpu.SMEM),
            hbm,
            hbm,
            hbm,
            vmem,
        ],
        out_specs=hbm,
        scratch_shapes=[
            pltpu.VMEM((BLK_DEV, OBS, TILE), BF16),
            pltpu.VMEM((BLK_DEV * 2 * SLAB_DEV, TILE), F32),
            pltpu.VMEM((SLAB_DEV, n_src, cap + 8, TILE), F32),
            pltpu.VMEM((SLAB_DEV, n_src, cap + 8, TILE), F32),
            pltpu.VMEM((TILES, n_src * cap), BF16),
            pltpu.VMEM((SLAB_DEV, LAT_DEV, NLON + 2 * TILE), F32),
            pltpu.VMEM((SLAB_DEV, SPAN, NLON), F32),
            pltpu.VMEM((TAPS, NLON), F32),
            pltpu.VMEM((SLAB_DEV, LAT_DEV, NLON), F32),
            dma((W_PARTS,)),
            dma((SLAB_DEV,)),
            dma,
            dma((SLAB_DEV,)),
            dma((SLAB_DEV, n_src)),
            dma((SLAB_DEV, n_src)),
            dma((SLAB_DEV, 2)),
            dma((SLAB_DEV, 2)),
        ],
        compiler_params=pltpu.CompilerParams(
            collective_id=0, has_side_effects=True, vmem_limit_bytes=40 << 20
        ),
    )(
        departures,
        destinations,
        tile_index.reshape(1, BLK_DEV),
        obs_count,
        interp_weights,
        background,
        lon_taps,
        lat_taps,
    )


def solution(mesh):
    return jax.shard_map(
        on_device,
        mesh=mesh,
        in_specs=(
            P(("groups", "band", "rd"), "lev", None),
            P(("groups", "band", "rd"), None),
            P(("groups", "band", "rd")),
            P(("groups", "band", "rd")),
            P(("groups", "band", "rd"), None, None),
            P(("groups", "lev", "rd"), "band", None),
            P(),
            P(),
        ),
        out_specs=P(("groups", "lev", "rd"), "band", None),
        check_vma=False,
    )
```

```python
import functools

import jax
import jax.numpy as jnp
from jax import lax
from jax.experimental import pallas as pl
from jax.experimental.pallas import tpu as pltpu
from jax.sharding import PartitionSpec as P

NLON = 7168
OBS = 128
TILE = 128
REACH = 8
SLAB_DEV = 2
LAT_DEV = 16
BLK_DEV = 128
ROW_TILES = NLON // TILE
TILES = ROW_TILES * LAT_DEV
TAPS = 2 * REACH + 1
SPAN = LAT_DEV + 2 * REACH
W_PARTS = 4
CHUNK_TILES = 7
CHUNK = CHUNK_TILES * TILE
CHUNKS = NLON // CHUNK
F32 = jnp.float32
BF16 = jnp.bfloat16
MESH = pl.DeviceIdType.MESH


def iota(shape, axis):
    return lax.broadcasted_iota(jnp.int32, shape, axis)


def split(value):
    high = value.astype(BF16)
    return high, (value - high.astype(F32)).astype(BF16)


def kernel(
    n_band,
    n_rd,
    cap,
    dep_ref,
    dest_ref,
    tile_ref,
    count_ref,
    w_hbm,
    bg_hbm,
    lon_hbm,
    lat_ref,
    out_hbm,
    w_v,
    masked,
    values,
    outbox,
    inbox,
    onehot,
    field,
    along,
    lon_v,
    out_v,
    w_sem,
    bg_sem,
    lon_sem,
    out_sem,
    box_send,
    box_recv,
    halo_send,
    halo_recv,
):
    n_src = n_band * n_rd
    slots = n_band * cap
    per_group = TILE // cap
    groups = n_src // per_group
    band = lax.axis_index("band")
    rd = lax.axis_index("rd")
    me = band * n_rd + rd

    w_copies = []
    part = BLK_DEV // W_PARTS
    for i in range(W_PARTS):
        rows = pl.ds(i * part, part)
        w_copies.append(pltpu.make_async_copy(w_hbm.at[rows], w_v.at[rows], w_sem.at[i]))
        w_copies[-1].start()
    bg_copies = []
    for s in range(SLAB_DEV):
        bg_copies.append(
            pltpu.make_async_copy(
                bg_hbm.at[s], field.at[s, :, pl.ds(TILE, NLON)], bg_sem.at[s]
            )
        )
        bg_copies[-1].start()
    lon_copy = pltpu.make_async_copy(lon_hbm, lon_v, lon_sem)
    lon_copy.start()

    barrier = pltpu.get_barrier_semaphore()

    def greet(step, carry):
        other = lax.rem(me + step, n_src)
        pl.semaphore_signal(
            barrier,
            inc=1,
            device_id={"band": other // n_rd, "rd": lax.rem(other, n_rd)},
            device_id_type=MESH,
        )
        return carry

    lax.fori_loop(1, n_src, greet, 0)

    square = (BLK_DEV, BLK_DEV)
    lane, sub = iota(square, 1), iota(square, 0)
    eye = lane == sub


    def column(row):
        return jnp.sum(jnp.where(eye, row.astype(F32), 0.0), axis=1, keepdims=True)

    dest_column = column(dest_ref[...])
    dest = jnp.broadcast_to(dest_column, square).astype(jnp.int32)
    chosen = (dest == lane).astype(F32)
    before = (lane < sub).astype(BF16)
    earlier = jnp.dot(before, chosen.astype(BF16), preferred_element_type=F32)
    rank = jnp.sum(earlier * chosen, axis=1, keepdims=True)
    slot = dest_column * cap + rank
    slot_row = jnp.sum(jnp.where(eye, slot, 0.0), axis=0, keepdims=True)
    pack = (iota((slots, BLK_DEV), 0).astype(F32) == slot_row).astype(BF16)
    tile_row = tile_ref[...]
    lat_row = jnp.zeros_like(tile_row)
    for r in range(1, LAT_DEV):
        lat_row = lat_row + (tile_row >= r * ROW_TILES).astype(jnp.int32)
    place_row = (tile_row - lat_row * ROW_TILES) * LAT_DEV + lat_row + 1
    place = column(place_row)
    shift = lax.rem(me, per_group) * cap
    lane_at = (lane - shift).astype(F32)
    label_of = jnp.where(lane_at == rank, place, 0.0)
    for d in range(n_band):
        row = jnp.sum(jnp.where(dest == d, label_of, 0.0), axis=0, keepdims=True)
        row = jnp.broadcast_to(row, (8, TILE))
        for r in range(n_rd):
            outbox[0, d * n_rd + r, pl.ds(cap, 8), :] = row

    height = 2 * SLAB_DEV
    rows_of = (BLK_DEV * height, BLK_DEV)
    picked = jnp.where(
        iota(rows_of, 0) // height == iota(rows_of, 1), count_ref[...].astype(F32), 0.0
    )
    counts = jnp.sum(picked, axis=1, keepdims=True)
    wide_dep = dep_ref[...].astype(F32).reshape(rows_of)
    masked[...] = jnp.where(iota(rows_of, 1).astype(F32) < counts, wide_dep, 0.0)
    first = iota((4 * height, OBS), 0) % (2 * height) < height
    for i in range(W_PARTS):
        w_copies[i].wait()

        def multiply(group, carry):
            at = pl.multiple_of(group * 4 * height, 4 * height)
            obs = masked[pl.ds(at, 4 * height), :]
            left = jnp.concatenate(
                [jnp.where(first, obs, 0.0), jnp.where(first, 0.0, obs)], axis=1
            ).astype(BF16)
            right = jnp.concatenate(
                [
                    w_v[pl.ds(group * 4, 2)].reshape(2 * OBS, TILE),
                    w_v[pl.ds(group * 4 + 2, 2)].reshape(2 * OBS, TILE),
                ],
                axis=1,
            )
            product = jnp.dot(left, right, preferred_element_type=F32)
            values[pl.ds(at, 2 * height), :] = product[: 2 * height, :TILE]
            values[pl.ds(at + 2 * height, 2 * height), :] = product[2 * height :, TILE:]
            return carry

        lax.fori_loop(i * part // 4, (i + 1) * part // 4, multiply, 0, unroll=4)

    pl.semaphore_wait(barrier, n_src - 1)

    def box_copy(s, step):
        other = lax.rem(me + step, n_src)
        size = cap + 8 if s == 0 else cap
        return pltpu.make_async_remote_copy(
            src_ref=outbox.at[s, other, pl.ds(0, size)],
            dst_ref=inbox.at[s, me, pl.ds(0, size)],
            send_sem=box_send.at[s, step],
            recv_sem=box_recv.at[s, step],
            device_id={"band": other // n_rd, "rd": lax.rem(other, n_rd)},
            device_id_type=MESH,
        )

    for s in range(SLAB_DEV):
        for r in range(n_rd):
            value = values[pl.ds(r * SLAB_DEV + s, BLK_DEV, stride=2 * SLAB_DEV), :]
            both = jnp.dot(
                pack, jnp.concatenate(split(value), axis=1), preferred_element_type=F32
            )
            both = both[:, :TILE] + both[:, TILE:]
            for d in range(n_band):
                outbox[s, d * n_rd + r, pl.ds(0, cap), :] = both[d * cap : (d + 1) * cap]

        def send(step, carry, s=s):
            box_copy(s, step).start()
            return carry

        lax.fori_loop(1, n_src, send, 0)
        inbox[s, me] = outbox[s, me]

    n_lat = lat_ref.shape[1]
    wide = (LAT_DEV, 128)
    own = iota((LAT_DEV, n_lat), 1) == iota((LAT_DEV, n_lat), 0) + band * LAT_DEV
    lane16, sub16 = iota(wide, 1), iota(wide, 0)
    third = lane16 // SPAN
    offset = lane16 - third * SPAN - sub16
    lat_matrix = jnp.zeros(wide, F32)
    for k in range(TAPS):
        tap = jnp.sum(jnp.where(own, lat_ref[k : k + 1, :], 0.0), axis=1, keepdims=True)
        lat_matrix = lat_matrix + jnp.where(offset == k, tap, 0.0)
    high = lat_matrix.astype(BF16).astype(F32)
    lat_matrix = jnp.where(third == 1, lat_matrix - high, high).astype(BF16)[:, : 3 * SPAN]

    @pl.when(band == 0)
    def _():
        along[:, pl.ds(0, REACH), :] = jnp.zeros((SLAB_DEV, REACH, NLON), F32)

    @pl.when(band == n_band - 1)
    def _():
        along[:, pl.ds(REACH + LAT_DEV, REACH), :] = jnp.zeros((SLAB_DEV, REACH, NLON), F32)

    def halo_copy(s, up):
        source = LAT_DEV if up else REACH
        target = 0 if up else REACH + LAT_DEV
        return pltpu.make_async_remote_copy(
            src_ref=along.at[s, pl.ds(source, REACH)],
            dst_ref=along.at[s, pl.ds(target, REACH)],
            send_sem=halo_send.at[s, int(up)],
            recv_sem=halo_recv.at[s, int(up)],
            device_id={"band": band + 1 if up else band - 1, "rd": rd},
            device_id_type=MESH,
        )

    for s in range(SLAB_DEV):

        def take(step, carry, s=s):
            box_copy(s, step).wait_recv()
            return carry

        bg_copies[s].wait()
        lax.fori_loop(1, n_src, take, 0)
        if s == 0:
            rows = iota((CHUNK_TILES * LAT_DEV, TILE), 0) + 1
            for g in range(groups):
                label = jnp.sum(
                    inbox[0, pl.ds(g * per_group, per_group), cap, :], axis=0, keepdims=True
                )

                def mark(c, carry, g=g, label=label):
                    at = pl.multiple_of(c * CHUNK_TILES * LAT_DEV, 16)
                    hit = (rows + at).astype(F32) == label
                    onehot[pl.ds(at, CHUNK_TILES * LAT_DEV), pl.ds(g * TILE, TILE)] = hit.astype(
                        F32
                    ).astype(BF16)
                    return carry

                lax.fori_loop(0, CHUNKS, mark, 0)
            lon_copy.wait()
        received = inbox[s, :, pl.ds(0, cap), :].reshape(n_src * cap, TILE)
        pieces = jnp.concatenate(split(received), axis=1)

        def add(c, carry, s=s, pieces=pieces):
            at = pl.multiple_of(c * CHUNK_TILES * LAT_DEV, 16)
            both = jnp.dot(
                onehot[pl.ds(at, CHUNK_TILES * LAT_DEV), :], pieces, preferred_element_type=F32
            )
            both = both[:, :TILE] + both[:, TILE:]
            for q in range(CHUNK_TILES):
                columns = pl.ds(pl.multiple_of((c * CHUNK_TILES + q + 1) * TILE, TILE), TILE)
                field[s, :, columns] += both[q * LAT_DEV : (q + 1) * LAT_DEV]
            return carry

        lax.fori_loop(0, CHUNKS, add, 0)
        field[s, :, pl.ds(0, TILE)] = field[s, :, pl.ds(NLON, TILE)]
        field[s, :, pl.ds(NLON + TILE, TILE)] = field[s, :, pl.ds(TILE, TILE)]

        def lon_filter(c, carry, s=s):
            at = pl.multiple_of(c * CHUNK, TILE)
            width = CHUNK + 2 * TILE
            window = field[s, :, pl.ds(at, width)]
            total = jnp.zeros((LAT_DEV, CHUNK), F32)
            for k in range(TAPS):
                moved = window if k == REACH else pltpu.roll(window, (REACH - k) % width, 1)
                total = total + lon_v[k : k + 1, pl.ds(at, CHUNK)] * moved[:, TILE : TILE + CHUNK]
            along[s, pl.ds(REACH, LAT_DEV), pl.ds(at, CHUNK)] = total
            return carry

        lax.fori_loop(0, CHUNKS, lon_filter, 0)

        @pl.when(band < n_band - 1)
        def _(s=s):
            halo_copy(s, True).start()

        @pl.when(band > 0)
        def _(s=s):
            halo_copy(s, False).start()

    out_copies = []
    for s in range(SLAB_DEV):

        @pl.when(band > 0)
        def _(s=s):
            halo_copy(s, True).wait_recv()

        @pl.when(band < n_band - 1)
        def _(s=s):
            halo_copy(s, False).wait_recv()

        def lat_filter(c, carry, s=s):
            columns = pl.ds(pl.multiple_of(c * CHUNK, TILE), CHUNK)
            high, low = split(along[s, :, columns])
            out_v[s, :, columns] = jnp.dot(
                lat_matrix,
                jnp.concatenate([high, high, low], axis=0),
                preferred_element_type=F32,
            )
            return carry

        lax.fori_loop(0, CHUNKS, lat_filter, 0)
        out_copies.append(pltpu.make_async_copy(out_v.at[s], out_hbm.at[s], out_sem.at[s]))
        out_copies[-1].start()

    for s in range(SLAB_DEV):

        def sent(step, carry, s=s):
            box_copy(s, step).wait_send()
            return carry

        lax.fori_loop(1, n_src, sent, 0)

        @pl.when(band < n_band - 1)
        def _(s=s):
            halo_copy(s, True).wait_send()

        @pl.when(band > 0)
        def _(s=s):
            halo_copy(s, False).wait_send()

        out_copies[s].wait()


def on_device(
    departures, destinations, tile_index, obs_count, interp_weights, background, lon_taps, lat_taps
):
    n_band = lax.axis_size("band")
    n_rd = lax.axis_size("rd")
    cap = max(2, 2 * BLK_DEV // n_band)
    n_src = n_band * n_rd
    vmem = pl.BlockSpec(memory_space=pltpu.VMEM)
    hbm = pl.BlockSpec(memory_space=pltpu.HBM)
    dma = pltpu.SemaphoreType.DMA
    return pl.pallas_call(
        functools.partial(kernel, n_band, n_rd, cap),
        out_shape=jax.ShapeDtypeStruct(background.shape, F32),
        in_specs=[
            vmem,
            vmem,
            vmem,
            vmem,
            hbm,
            hbm,
            hbm,
            vmem,
        ],
        out_specs=hbm,
        scratch_shapes=[
            pltpu.VMEM((BLK_DEV, OBS, TILE), BF16),
            pltpu.VMEM((BLK_DEV * 2 * SLAB_DEV, OBS), F32),
            pltpu.VMEM((BLK_DEV * 2 * SLAB_DEV, TILE), F32),
            pltpu.VMEM((SLAB_DEV, n_src, cap + 8, TILE), F32),
            pltpu.VMEM((SLAB_DEV, n_src, cap + 8, TILE), F32),
            pltpu.VMEM((TILES, n_src * cap), BF16),
            pltpu.VMEM((SLAB_DEV, LAT_DEV, NLON + 2 * TILE), F32),
            pltpu.VMEM((SLAB_DEV, SPAN, NLON), F32),
            pltpu.VMEM((TAPS, NLON), F32),
            pltpu.VMEM((SLAB_DEV, LAT_DEV, NLON), F32),
            dma((W_PARTS,)),
            dma((SLAB_DEV,)),
            dma,
            dma((SLAB_DEV,)),
            dma((SLAB_DEV, n_src)),
            dma((SLAB_DEV, n_src)),
            dma((SLAB_DEV, 2)),
            dma((SLAB_DEV, 2)),
        ],
        compiler_params=pltpu.CompilerParams(
            collective_id=0, has_side_effects=True, vmem_limit_bytes=56 << 20
        ),
    )(
        departures,
        destinations.reshape(1, BLK_DEV),
        tile_index.reshape(1, BLK_DEV),
        obs_count.reshape(1, BLK_DEV),
        interp_weights,
        background,
        lon_taps,
        lat_taps,
    )


def solution(mesh):
    return jax.shard_map(
        on_device,
        mesh=mesh,
        in_specs=(
            P(("groups", "band", "rd"), "lev", None),
            P(("groups", "band", "rd"), None),
            P(("groups", "band", "rd")),
            P(("groups", "band", "rd")),
            P(("groups", "band", "rd"), None, None),
            P(("groups", "lev", "rd"), "band", None),
            P(),
            P(),
        ),
        out_specs=P(("groups", "lev", "rd"), "band", None),
        check_vma=False,
    )
```

```python
import functools

import jax
import jax.numpy as jnp
from jax import lax
from jax.experimental import pallas as pl
from jax.experimental.pallas import tpu as pltpu
from jax.sharding import PartitionSpec as P

NLON = 7168
OBS = 128
TILE = 128
REACH = 8
SLAB_DEV = 2
LAT_DEV = 16
BLK_DEV = 128
ROW_TILES = NLON // TILE
TILES = ROW_TILES * LAT_DEV
TAPS = 2 * REACH + 1
SPAN = LAT_DEV + 2 * REACH
W_PARTS = 4
CHUNK_TILES = 7
CHUNK = CHUNK_TILES * TILE
CHUNKS = NLON // CHUNK
PIECES = 4
PIECE_CHUNKS = CHUNKS // PIECES
PIECE = CHUNK * PIECE_CHUNKS
F32 = jnp.float32
BF16 = jnp.bfloat16
MESH = pl.DeviceIdType.MESH


def iota(shape, axis):
    return lax.broadcasted_iota(jnp.int32, shape, axis)


def split(value):
    high = value.astype(BF16)
    return high, (value - high.astype(F32)).astype(BF16)


def kernel(
    n_band,
    n_rd,
    cap,
    dep_ref,
    dest_ref,
    tile_ref,
    count_ref,
    w_hbm,
    bg_hbm,
    lon_hbm,
    lat_ref,
    out_v,
    w_v,
    masked,
    values,
    outbox,
    inbox,
    onehot,
    field,
    along,
    lon_v,
    w_sem,
    bg_sem,
    lon_sem,
    box_send,
    box_recv,
    halo_send,
    halo_recv,
):
    n_src = n_band * n_rd
    slots = n_band * cap
    per_group = TILE // cap
    groups = n_src // per_group
    band = lax.axis_index("band")
    rd = lax.axis_index("rd")
    me = band * n_rd + rd

    w_copies = []
    part = BLK_DEV // W_PARTS
    for i in range(W_PARTS):
        rows = pl.ds(i * part, part)
        w_copies.append(pltpu.make_async_copy(w_hbm.at[rows], w_v.at[rows], w_sem.at[i]))
        w_copies[-1].start()
    bg_copies = []
    for s in range(SLAB_DEV):
        bg_copies.append(
            pltpu.make_async_copy(
                bg_hbm.at[s], field.at[s, :, pl.ds(TILE, NLON)], bg_sem.at[s]
            )
        )
        bg_copies[-1].start()
    lon_copy = pltpu.make_async_copy(lon_hbm, lon_v, lon_sem)
    lon_copy.start()

    barrier = pltpu.get_barrier_semaphore()

    def greet(step, carry):
        other = lax.rem(me + step, n_src)
        pl.semaphore_signal(
            barrier,
            inc=1,
            device_id={"band": other // n_rd, "rd": lax.rem(other, n_rd)},
            device_id_type=MESH,
        )
        return carry

    lax.fori_loop(1, n_src, greet, 0)

    square = (BLK_DEV, BLK_DEV)
    lane, sub = iota(square, 1), iota(square, 0)
    eye = lane == sub


    def column(row):
        return jnp.sum(jnp.where(eye, row.astype(F32), 0.0), axis=1, keepdims=True)

    dest_column = column(dest_ref[...])
    dest = jnp.broadcast_to(dest_column, square).astype(jnp.int32)
    chosen = (dest == lane).astype(F32)
    before = (lane < sub).astype(BF16)
    earlier = jnp.dot(before, chosen.astype(BF16), preferred_element_type=F32)
    rank = jnp.sum(earlier * chosen, axis=1, keepdims=True)
    slot = dest_column * cap + rank
    slot_row = jnp.sum(jnp.where(eye, slot, 0.0), axis=0, keepdims=True)
    pack = (iota((slots, BLK_DEV), 0).astype(F32) == slot_row).astype(BF16)
    tile_row = tile_ref[...]
    lat_row = jnp.zeros_like(tile_row)
    for r in range(1, LAT_DEV):
        lat_row = lat_row + (tile_row >= r * ROW_TILES).astype(jnp.int32)
    place_row = (tile_row - lat_row * ROW_TILES) * LAT_DEV + lat_row + 1
    place = column(place_row)
    shift = lax.rem(me, per_group) * cap
    lane_at = (lane - shift).astype(F32)
    label_of = jnp.where(lane_at == rank, place, 0.0)
    for d in range(n_band):
        row = jnp.sum(jnp.where(dest == d, label_of, 0.0), axis=0, keepdims=True)
        row = jnp.broadcast_to(row, (8, TILE))
        for r in range(n_rd):
            outbox[0, d * n_rd + r, pl.ds(cap, 8), :] = row

    height = 2 * SLAB_DEV
    rows_of = (BLK_DEV * height, BLK_DEV)
    picked = jnp.where(
        iota(rows_of, 0) // height == iota(rows_of, 1), count_ref[...].astype(F32), 0.0
    )
    counts = jnp.sum(picked, axis=1, keepdims=True)
    wide_dep = dep_ref[...].astype(F32).reshape(rows_of)
    masked[...] = jnp.where(iota(rows_of, 1).astype(F32) < counts, wide_dep, 0.0)
    first = iota((4 * height, OBS), 0) % (2 * height) < height
    for i in range(W_PARTS):
        w_copies[i].wait()

        def multiply(group, carry):
            at = pl.multiple_of(group * 4 * height, 4 * height)
            obs = masked[pl.ds(at, 4 * height), :]
            left = jnp.concatenate(
                [jnp.where(first, obs, 0.0), jnp.where(first, 0.0, obs)], axis=1
            ).astype(BF16)
            right = jnp.concatenate(
                [
                    w_v[pl.ds(group * 4, 2)].reshape(2 * OBS, TILE),
                    w_v[pl.ds(group * 4 + 2, 2)].reshape(2 * OBS, TILE),
                ],
                axis=1,
            )
            product = jnp.dot(left, right, preferred_element_type=F32)
            values[pl.ds(at, 2 * height), :] = product[: 2 * height, :TILE]
            values[pl.ds(at + 2 * height, 2 * height), :] = product[2 * height :, TILE:]
            return carry

        lax.fori_loop(i * part // 4, (i + 1) * part // 4, multiply, 0, unroll=4)

    pl.semaphore_wait(barrier, n_src - 1)

    def box_copy(s, step):
        other = lax.rem(me + step, n_src)
        size = cap + 8 if s == 0 else cap
        return pltpu.make_async_remote_copy(
            src_ref=outbox.at[s, other, pl.ds(0, size)],
            dst_ref=inbox.at[s, me, pl.ds(0, size)],
            send_sem=box_send.at[s, step],
            recv_sem=box_recv.at[s, step],
            device_id={"band": other // n_rd, "rd": lax.rem(other, n_rd)},
            device_id_type=MESH,
        )

    for s in range(SLAB_DEV):
        for r in range(n_rd):
            value = values[pl.ds(r * SLAB_DEV + s, BLK_DEV, stride=2 * SLAB_DEV), :]
            both = jnp.dot(
                pack, jnp.concatenate(split(value), axis=1), preferred_element_type=F32
            )
            both = both[:, :TILE] + both[:, TILE:]
            for d in range(n_band):
                outbox[s, d * n_rd + r, pl.ds(0, cap), :] = both[d * cap : (d + 1) * cap]

        def send(step, carry, s=s):
            box_copy(s, step).start()
            return carry

        lax.fori_loop(1, n_src, send, 0)
        inbox[s, me] = outbox[s, me]

    n_lat = lat_ref.shape[1]
    wide = (LAT_DEV, 128)
    own = iota((LAT_DEV, n_lat), 1) == iota((LAT_DEV, n_lat), 0) + band * LAT_DEV
    lane16, sub16 = iota(wide, 1), iota(wide, 0)
    third = lane16 // SPAN
    offset = lane16 - third * SPAN - sub16
    lat_matrix = jnp.zeros(wide, F32)
    for k in range(TAPS):
        tap = jnp.sum(jnp.where(own, lat_ref[k : k + 1, :], 0.0), axis=1, keepdims=True)
        lat_matrix = lat_matrix + jnp.where(offset == k, tap, 0.0)
    high = lat_matrix.astype(BF16).astype(F32)
    lat_matrix = jnp.where(third == 1, lat_matrix - high, high).astype(BF16)[:, : 3 * SPAN]

    @pl.when(band == 0)
    def _():
        along[:, pl.ds(0, REACH), :] = jnp.zeros((SLAB_DEV, REACH, NLON), F32)

    @pl.when(band == n_band - 1)
    def _():
        along[:, pl.ds(REACH + LAT_DEV, REACH), :] = jnp.zeros((SLAB_DEV, REACH, NLON), F32)

    def halo_copy(s, h, up):
        columns = pl.ds(h * PIECE, PIECE)
        source = LAT_DEV if up else REACH
        target = 0 if up else REACH + LAT_DEV
        return pltpu.make_async_remote_copy(
            src_ref=along.at[s, pl.ds(source, REACH), columns],
            dst_ref=along.at[s, pl.ds(target, REACH), columns],
            send_sem=halo_send.at[s, h, int(up)],
            recv_sem=halo_recv.at[s, h, int(up)],
            device_id={"band": band + 1 if up else band - 1, "rd": rd},
            device_id_type=MESH,
        )

    for s in range(SLAB_DEV):

        def take(step, carry, s=s):
            box_copy(s, step).wait_recv()
            return carry

        bg_copies[s].wait()
        lax.fori_loop(1, n_src, take, 0)
        if s == 0:
            rows = iota((CHUNK_TILES * LAT_DEV, TILE), 0) + 1
            for g in range(groups):
                label = jnp.sum(
                    inbox[0, pl.ds(g * per_group, per_group), cap, :], axis=0, keepdims=True
                )

                def mark(c, carry, g=g, label=label):
                    at = pl.multiple_of(c * CHUNK_TILES * LAT_DEV, 16)
                    hit = (rows + at).astype(F32) == label
                    onehot[pl.ds(at, CHUNK_TILES * LAT_DEV), pl.ds(g * TILE, TILE)] = hit.astype(
                        F32
                    ).astype(BF16)
                    return carry

                lax.fori_loop(0, CHUNKS, mark, 0)
            lon_copy.wait()
        received = inbox[s, :, pl.ds(0, cap), :].reshape(n_src * cap, TILE)
        pieces = jnp.concatenate(split(received), axis=1)

        def add(c, carry, s=s, pieces=pieces):
            at = pl.multiple_of(c * CHUNK_TILES * LAT_DEV, 16)
            both = jnp.dot(
                onehot[pl.ds(at, CHUNK_TILES * LAT_DEV), :], pieces, preferred_element_type=F32
            )
            both = both[:, :TILE] + both[:, TILE:]
            for q in range(CHUNK_TILES):
                columns = pl.ds(pl.multiple_of((c * CHUNK_TILES + q + 1) * TILE, TILE), TILE)
                field[s, :, columns] += both[q * LAT_DEV : (q + 1) * LAT_DEV]
            return carry

        lax.fori_loop(0, CHUNKS, add, 0)
        field[s, :, pl.ds(0, TILE)] = field[s, :, pl.ds(NLON, TILE)]
        field[s, :, pl.ds(NLON + TILE, TILE)] = field[s, :, pl.ds(TILE, TILE)]

        def lon_filter(c, carry, s=s):
            at = pl.multiple_of(c * CHUNK, TILE)
            width = CHUNK + 2 * TILE
            window = field[s, :, pl.ds(at, width)]
            total = jnp.zeros((LAT_DEV, CHUNK), F32)
            for k in range(TAPS):
                moved = window if k == REACH else pltpu.roll(window, (REACH - k) % width, 1)
                total = total + lon_v[k : k + 1, pl.ds(at, CHUNK)] * moved[:, TILE : TILE + CHUNK]
            along[s, pl.ds(REACH, LAT_DEV), pl.ds(at, CHUNK)] = total
            return carry

        for h in range(PIECES):
            lax.fori_loop(h * PIECE_CHUNKS, (h + 1) * PIECE_CHUNKS, lon_filter, 0)

            @pl.when(band < n_band - 1)
            def _(s=s, h=h):
                halo_copy(s, h, True).start()

            @pl.when(band > 0)
            def _(s=s, h=h):
                halo_copy(s, h, False).start()

    for s in range(SLAB_DEV):

        def lat_filter(c, carry, s=s):
            columns = pl.ds(pl.multiple_of(c * CHUNK, TILE), CHUNK)
            high, low = split(along[s, :, columns])
            out_v[s, :, columns] = jnp.dot(
                lat_matrix,
                jnp.concatenate([high, high, low], axis=0),
                preferred_element_type=F32,
            )
            return carry

        for h in range(PIECES):

            @pl.when(band > 0)
            def _(s=s, h=h):
                halo_copy(s, h, True).wait_recv()

            @pl.when(band < n_band - 1)
            def _(s=s, h=h):
                halo_copy(s, h, False).wait_recv()

            lax.fori_loop(h * PIECE_CHUNKS, (h + 1) * PIECE_CHUNKS, lat_filter, 0)

    for s in range(SLAB_DEV):

        def sent(step, carry, s=s):
            box_copy(s, step).wait_send()
            return carry

        lax.fori_loop(1, n_src, sent, 0)
        for h in range(PIECES):

            @pl.when(band < n_band - 1)
            def _(s=s, h=h):
                halo_copy(s, h, True).wait_send()

            @pl.when(band > 0)
            def _(s=s, h=h):
                halo_copy(s, h, False).wait_send()


def on_device(
    departures, destinations, tile_index, obs_count, interp_weights, background, lon_taps, lat_taps
):
    n_band = lax.axis_size("band")
    n_rd = lax.axis_size("rd")
    cap = max(2, 2 * BLK_DEV // n_band)
    n_src = n_band * n_rd
    vmem = pl.BlockSpec(memory_space=pltpu.VMEM)
    hbm = pl.BlockSpec(memory_space=pltpu.HBM)
    dma = pltpu.SemaphoreType.DMA
    return pl.pallas_call(
        functools.partial(kernel, n_band, n_rd, cap),
        out_shape=pltpu.VMEM(background.shape, F32),
        in_specs=[
            vmem,
            vmem,
            vmem,
            vmem,
            hbm,
            hbm,
            hbm,
            vmem,
        ],
        out_specs=pl.BlockSpec(memory_space=pltpu.VMEM),
        scratch_shapes=[
            pltpu.VMEM((BLK_DEV, OBS, TILE), BF16),
            pltpu.VMEM((BLK_DEV * 2 * SLAB_DEV, OBS), F32),
            pltpu.VMEM((BLK_DEV * 2 * SLAB_DEV, TILE), F32),
            pltpu.VMEM((SLAB_DEV, n_src, cap + 8, TILE), F32),
            pltpu.VMEM((SLAB_DEV, n_src, cap + 8, TILE), F32),
            pltpu.VMEM((TILES, n_src * cap), BF16),
            pltpu.VMEM((SLAB_DEV, LAT_DEV, NLON + 2 * TILE), F32),
            pltpu.VMEM((SLAB_DEV, SPAN, NLON), F32),
            pltpu.VMEM((TAPS, NLON), F32),
            dma((W_PARTS,)),
            dma((SLAB_DEV,)),
            dma,
            dma((SLAB_DEV, n_src)),
            dma((SLAB_DEV, n_src)),
            dma((SLAB_DEV, PIECES, 2)),
            dma((SLAB_DEV, PIECES, 2)),
        ],
        compiler_params=pltpu.CompilerParams(
            collective_id=0, has_side_effects=True, vmem_limit_bytes=56 << 20
        ),
    )(
        departures,
        destinations.reshape(1, BLK_DEV),
        tile_index.reshape(1, BLK_DEV),
        obs_count.reshape(1, BLK_DEV),
        interp_weights,
        background,
        lon_taps,
        lat_taps,
    )


def solution(mesh):
    return jax.shard_map(
        on_device,
        mesh=mesh,
        in_specs=(
            P(("groups", "band", "rd"), "lev", None),
            P(("groups", "band", "rd"), None),
            P(("groups", "band", "rd")),
            P(("groups", "band", "rd")),
            P(("groups", "band", "rd"), None, None),
            P(("groups", "lev", "rd"), "band", None),
            P(),
            P(),
        ),
        out_specs=P(("groups", "lev", "rd"), "band", None),
        check_vma=False,
    )
```
